512 devices in a mesh: gx: 32 (over z, y_hi), gy: 16 (over x, y_lo, core).
Axes of the slice: x: 4, y: 4 (y_hi: 2, y_lo: 2; y = y_hi * 2 + y_lo), z: 16, core: 2. Of those that a mesh axis runs over, the one named last changes fastest.
Arguments:
- disp: float32 [2, 1024, 2048], P(None, 'gx', 'gy'), may hold values from -0.1 to 0.1
- vel: float32 [2, 1024, 2048], P(None, 'gx', 'gy'), may hold values from -1.5 to 1.5
- stiffness: float32 [1024, 2048], P('gx', 'gy'), may hold values from 2 to 20
- body_force: float32 [2, 1024, 2048], P(None, 'gx', 'gy'), may hold values from -6 to 6
- bond_bits: int32 [2, 1024, 2048], P(None, 'gx', 'gy'), may hold values from 0 to 16383, as said below
Outputs:
- disp_final: float32 [2, 1024, 2048], P(None, 'gx', 'gy')
- vel_final: float32 [2, 1024, 2048], P(None, 'gx', 'gy')
The draws below stay inside these ranges and needn't reach their ends.
Inputs may be any that keep to these rules, and one draw needn't show every extreme that they name: `bond_bits`: bit j of word 0 of a point (j below 14) is 1 where its bond to offset j of the upper shell exists, bit j of word 1 where its bond to the mirrored offset exists; both ends of a bond carry the same flag, bonds that leave the plate are absent, and bits 14 and above are 0.
All inputs are finite; a program needn't handle non-finite values.
Results may differ from the reference program's by a relative error of at most 0.000026.
Values sent between devices are 32-bit elements; how exact they have to be, the bound alone decides.
A program may use at most 64 MiB of HBM per device.

```python
import math
import jax
import jax.numpy as jnp
from jax import lax

STEPS = 10
NX = 1024
NY = 2048


def upper_shell():
    upper = []
    for row_step in range(0, 4):
        for col_step in range(-3, 4):
            if row_step * row_step + col_step * col_step <= 9 and (row_step > 0 or col_step > 0):
                upper.append((row_step, col_step))
    return upper


def draw_bond_bits(key, part):
    key = jax.random.fold_in(key, 7)
    keep = (jax.random.randint(key, (14, NX, NY), 0, 4) < 3).astype(jnp.int32)
    row_index = jnp.arange(NX, dtype=jnp.int32)[:, None]
    col_index = jnp.arange(NY, dtype=jnp.int32)[None, :]
    upper_word = jnp.zeros((NX, NY), jnp.int32)
    lower_word = jnp.zeros((NX, NY), jnp.int32)
    for index, (row_step, col_step) in enumerate(upper_shell()):
        inside = ((row_index + row_step < NX) & (col_index + col_step >= 0) & (col_index + col_step < NY)).astype(jnp.int32)
        upper_bit = keep[index] * inside
        padded = jnp.pad(upper_bit, 3)
        lower_bit = padded[3 - row_step:3 - row_step + NX, 3 - col_step:3 - col_step + NY]
        upper_word = upper_word + upper_bit * 2 ** index
        lower_word = lower_word + lower_bit * 2 ** index
    return jnp.stack([upper_word, lower_word])


def levels(own_key, dims, pieces, least, largest):
    factor_of, own = 1.0, jax.random.fold_in(own_key, 6)
    for dim, blocks in pieces:
        draws = jnp.exp(jax.random.uniform(jax.random.fold_in(own, dim), (blocks,), jnp.float32, least / len(pieces), largest / len(pieces)))
        factor_of = factor_of * jnp.repeat(draws, dims[dim] // blocks).reshape([-1 if axis == dim else 1 for axis in range(len(dims))])
    return factor_of


def scatter_about(stream_key, shape, scale, limit, pieces=(), kind=jnp.bfloat16):
    array = jax.random.normal(stream_key, shape, jnp.float32) * scale
    if len(pieces) > 0:
        array = levels(stream_key, shape, pieces, -0.22, 0.18) * array
    return jnp.clip(array, min=-limit, max=limit).astype(kind)


def setup_inputs(seed: int = 0) -> dict:
    keys = jax.random.split(jax.random.key(seed), 6)
    disp = scatter_about(keys[0], (2, NX, NY), 0.03, 0.1, ((1, 32), (2, 16)), jnp.float32)
    vel = scatter_about(keys[1], (2, NX, NY), 0.3, 1.5, ((1, 32), (2, 16)), jnp.float32)
    stiffness = jnp.clip(jnp.exp(math.log(20.0) - 2.3025851 * jax.random.uniform(keys[2], (NX, NY), jnp.float32) ** levels(keys[2], (NX, NY), ((0, 32), (1, 16)), -0.2, 0.2)), 2.0, 20.0)
    body_force = scatter_about(keys[3], (2, NX, NY), 1.0, 6.0, ((1, 32), (2, 16)), jnp.float32)
    bond_bits = draw_bond_bits(jax.random.fold_in(keys[5], 71), 0)
    return {"disp": disp, "vel": vel, "stiffness": stiffness, "body_force": body_force, "bond_bits": bond_bits}


TIME_STEP = 0.04

def shell_offsets():
    upper = []
    for row_step in range(0, 4):
        for col_step in range(-3, 4):
            if row_step * row_step + col_step * col_step <= 9 and (row_step > 0 or col_step > 0):
                upper.append((row_step, col_step))
    return upper

def bond_term(itself, other, offset, bond_bits, index):
    row_step, col_step = offset
    spread_x = row_step + other[0] - itself[0]
    spread_y = col_step + other[1] - itself[1]
    length = math.sqrt(row_step * row_step + col_step * col_step)
    dist = jnp.sqrt(spread_x * spread_x + spread_y * spread_y)
    live = bond_bits[index // 14] // 2 ** (index % 14) % 2
    weight = 0.5 * (itself[2] + other[2]) * (dist - length) / (length * dist)
    weight = jnp.where(live == 1, weight, jnp.zeros_like(weight))
    return (weight * spread_x, weight * spread_y)

def plate_forces(disp, stiffness, bond_bits):
    rows_all, cols_all = stiffness.shape
    padded = [jnp.pad(disp[0], 3), jnp.pad(disp[1], 3), jnp.pad(stiffness, 3)]
    itself = (disp[0], disp[1], stiffness)
    upper = shell_offsets()
    offsets = upper + [(-row_step, -col_step) for row_step, col_step in upper]
    force_x = jnp.zeros_like(stiffness)
    force_y = jnp.zeros_like(stiffness)
    for index, (row_step, col_step) in enumerate(offsets):
        other = tuple((field[3 + row_step:3 + row_step + rows_all, 3 + col_step:3 + col_step + cols_all] for field in padded))
        term_x, term_y = bond_term(itself, other, (row_step, col_step), bond_bits, index)
        force_x = force_x + term_x
        force_y = force_y + term_y
    return jnp.stack([force_x, force_y])

def reference(disp, vel, stiffness, body_force, bond_bits):
    accel = plate_forces(disp, stiffness, bond_bits) + body_force

    def advance(step, carry):
        current, moving, accel_now = carry
        halfway = moving + 0.5 * TIME_STEP * accel_now
        current = current + TIME_STEP * halfway
        accel_next = plate_forces(current, stiffness, bond_bits) + body_force
        return (current, halfway + 0.5 * TIME_STEP * accel_next, accel_next)
    disp, vel, accel = lax.fori_loop(0, STEPS, advance, (disp, vel, accel))
    return (disp, vel)
```

```python
import functools
import math

import jax
import jax.numpy as jnp
from jax import lax
from jax.experimental import pallas as pl
from jax.experimental.pallas import tpu as pltpu
from jax.sharding import PartitionSpec as P

STEPS = 10
TIME_STEP = 0.04
ROWS = 32
COLS = 128
BASE = 48
TALL = 128
SIDE = 96
TINY = 1.2e-38
MESH = pl.DeviceIdType.MESH


def upper_shell():
    upper = []
    for row_step in range(0, 4):
        for col_step in range(-3, 4):
            if row_step * row_step + col_step * col_step <= 9 and (row_step > 0 or col_step > 0):
                upper.append((row_step, col_step))
    return upper


def half_shell():
    bonds = []
    for index, (row_step, col_step) in enumerate(upper_shell()):
        if col_step >= 0:
            bonds.append((row_step, col_step, index, False))
        else:
            bonds.append((-row_step, -col_step, index, True))
    return sorted(bonds, key=lambda bond: (bond[1], bond[0]))


BONDS = half_shell()


def lanes_of(shape):
    return lax.broadcasted_iota(jnp.int32, shape, len(shape) - 1)


def ahead(first, second, step):
    if step == 0:
        return first, second
    inside = lanes_of(first.shape) < COLS - step
    a, b = pltpu.roll(first, COLS - step, 1), pltpu.roll(second, COLS - step, 1)
    return jnp.where(inside, a, b), jnp.where(inside, b, a)


def behind(first, second, step):
    if step == 0:
        return first, second
    inside = lanes_of(first.shape) >= step
    a, b = pltpu.roll(first, step, 1), pltpu.roll(second, step, 1)
    return jnp.where(inside, a, b), jnp.where(inside, b, a)


def packed(fields, starts, group_starts):
    lanes = lanes_of((ROWS, COLS))
    total = None
    for field, start, group in zip(fields, starts, group_starts, strict=True):
        moved = pltpu.roll(field, (group - start) % COLS, 1)
        total = moved if total is None else jnp.where((lanes >= group) & (lanes < group + 32), moved, total)
    return total


def exchange_kernel(shape_x, shape_y, disp, vel, stiff, body, bits, ext, left, right,
                    bits_own, to_west, to_east, local_sem, send_sem, recv_sem):
    gx, gy = lax.axis_index("gx"), lax.axis_index("gy")

    def neighbour(row_step, col_step):
        return (
            lax.rem(gx + row_step + shape_x, shape_x),
            lax.rem(gy + col_step + shape_y, shape_y),
        )

    around = [(-1, 0), (1, 0), (0, -1), (0, 1), (-1, -1), (-1, 1), (1, -1), (1, 1), (-2, 0), (2, 0)]
    barrier = pltpu.get_barrier_semaphore()
    for step in around:
        pl.semaphore_signal(barrier, inc=1, device_id=neighbour(*step), device_id_type=MESH)

    own = pl.ds(BASE, ROWS)
    local = [
        pltpu.make_async_copy(bits.at[0], bits_own, local_sem.at[0]),
        pltpu.make_async_copy(disp, ext.at[pl.ds(0, 2), own], local_sem.at[1]),
        pltpu.make_async_copy(stiff, ext.at[2, own], local_sem.at[2]),
        pltpu.make_async_copy(vel, ext.at[pl.ds(4, 2), own], local_sem.at[3]),
        pltpu.make_async_copy(body, ext.at[pl.ds(6, 2), own], local_sem.at[4]),
    ]
    for copy in local:
        copy.start()
    for copy in local:
        copy.wait()
    ext[3, own] = bits_own[...].astype(jnp.float32)

    near = [ext[field, own] for field in range(8)]
    lanes = lanes_of((ROWS, COLS))
    groups = [0, 32, 64, 96]
    to_west[0] = packed(near[:4], [0] * 4, groups)
    to_east[0] = packed(near[:4], [96] * 4, groups)
    west, east = packed(near[4:], [0] * 4, groups), packed(near[4:], [96] * 4, groups)
    for field in range(4):
        group = groups[field]
        west = jnp.where(lanes == group + 30, pltpu.roll(near[field], (group + 30 - 32) % COLS, 1), west)
        east = jnp.where(lanes == group + 1, pltpu.roll(near[field], (group + 1 - 95) % COLS, 1), east)
    to_west[1] = west
    to_east[1] = east

    pl.semaphore_wait(barrier, len(around))

    near_fields, late_fields = pl.ds(0, 4), pl.ds(4, 4)
    plan = [
        (ext.at[near_fields, own], ext.at[near_fields, pl.ds(BASE + ROWS, ROWS)], (-1, 0)),
        (ext.at[near_fields, own], ext.at[near_fields, pl.ds(BASE - ROWS, ROWS)], (1, 0)),
        (to_west, right.at[:, pl.ds(64, 32)], (-1, -1)),
        (to_east, left.at[:, pl.ds(64, 32)], (-1, 1)),
        (to_west, right.at[:, pl.ds(0, 32)], (1, -1)),
        (to_east, left.at[:, pl.ds(0, 32)], (1, 1)),
        (to_west, right.at[:, pl.ds(32, 32)], (0, -1)),
        (to_east, left.at[:, pl.ds(32, 32)], (0, 1)),
        (ext.at[near_fields, pl.ds(BASE, 8)], ext.at[near_fields, pl.ds(BASE + 64, 8)], (-2, 0)),
        (ext.at[near_fields, pl.ds(BASE + 24, 8)], ext.at[near_fields, pl.ds(BASE - 40, 8)], (2, 0)),
        (ext.at[late_fields, own], ext.at[late_fields, pl.ds(BASE + ROWS, ROWS)], (-1, 0)),
        (ext.at[late_fields, own], ext.at[late_fields, pl.ds(BASE - ROWS, ROWS)], (1, 0)),
    ]
    copies = [
        pltpu.make_async_remote_copy(
            src_ref=source,
            dst_ref=target,
            send_sem=send_sem.at[index],
            recv_sem=recv_sem.at[index],
            device_id=neighbour(*step),
            device_id_type=MESH,
        )
        for index, (source, target, step) in enumerate(plan)
    ]
    for copy in copies:
        copy.start()
    for copy in copies:
        copy.wait_recv()
    for copy in copies:
        copy.wait_send()


def exchange(shape_x, shape_y, *args):
    any_space = pl.BlockSpec(memory_space=pl.ANY)
    vmem = pl.BlockSpec(memory_space=pltpu.VMEM)
    return pl.pallas_call(
        functools.partial(exchange_kernel, shape_x, shape_y),
        out_shape=(
            pltpu.VMEM((8, TALL, COLS), jnp.float32),
            pltpu.VMEM((2, SIDE, COLS), jnp.float32),
            pltpu.VMEM((2, SIDE, COLS), jnp.float32),
        ),
        in_specs=[any_space] * 5,
        out_specs=(vmem, vmem, vmem),
        scratch_shapes=[
            pltpu.VMEM((ROWS, COLS), jnp.int32),
            pltpu.VMEM((2, ROWS, COLS), jnp.float32),
            pltpu.VMEM((2, ROWS, COLS), jnp.float32),
            pltpu.SemaphoreType.DMA((5,)),
            pltpu.SemaphoreType.DMA((12,)),
            pltpu.SemaphoreType.DMA((12,)),
        ],
        compiler_params=pltpu.CompilerParams(collective_id=0, has_side_effects=True),
        name="exchange",
    )(*args)


def steps_kernel(ext, left, right, disp_out, vel_out, pos, half, push, coef, pair, near_sum, stiff, flags):
    lanes8 = lanes_of((8, COLS))
    low = lanes8 < 64

    def beside(word, group, rows):
        from_right = pltpu.roll(right[word, rows], (-32 * group) % COLS, 1)
        from_left = pltpu.roll(left[word, rows], (96 - 32 * group) % COLS, 1)
        return from_right, from_left

    def store_moved(buffer, rows, x, y):
        for step in range(4):
            mx, my = ahead(x[0], x[1], step), ahead(y[0], y[1], step)
            for tile in range(2):
                pos[buffer, 0, step, tile, rows] = mx[tile]
                pos[buffer, 1, step, tile, rows] = my[tile] + float(step) if step else my[tile]

    def set_up(index, carry):
        rows = pl.ds(pl.multiple_of(8 * index, 8), 8)
        side = pl.ds(pl.multiple_of(8 * index - 16, 8), 8)
        others = []
        for field in range(4):
            from_right, from_left = beside(0, field, side)
            value = jnp.where(lanes8 < 32, from_right, jnp.where(lanes8 >= 96, from_left, 0.0))
            far_right = pltpu.roll(right[1, side], (32 - (32 * field + 30)) % COLS, 1)
            far_left = pltpu.roll(left[1, side], (95 - (32 * field + 1)) % COLS, 1)
            value = jnp.where(lanes8 == 32, far_right, jnp.where(lanes8 == 95, far_left, value))
            others.append(value)
        own = [ext[field, rows] for field in range(4)]
        store_moved(0, rows, (own[0], others[0]), (own[1], others[1]))
        for step in range(4):
            moved = ahead(own[2], others[2], step)
            stiff[step, 0, rows], stiff[step, 1, rows] = moved
        for step in range(3):
            moved = ahead(own[3].astype(jnp.int32), others[3].astype(jnp.int32), step)
            flags[step, 0, rows], flags[step, 1, rows] = moved
        for component in range(2):
            half[component, 0, rows] = ext[4 + component, rows]
            push[component, 0, rows] = TIME_STEP * ext[6 + component, rows]
            from_right, from_left = beside(1, component, side)
            half[component, 1, rows] = jnp.where(lanes8 < 30, from_right, jnp.where(lanes8 >= 98, from_left, 0.0))
            from_right, from_left = beside(1, 2 + component, side)
            push[component, 1, rows] = TIME_STEP * jnp.where(
                lanes8 < 30, from_right, jnp.where(lanes8 >= 98, from_left, 0.0)
            )
        return carry

    zeros = jnp.zeros((8, COLS), jnp.float32)
    no_flags = jnp.zeros((8, COLS), jnp.int32)
    for index in (0, 1, 14, 15):
        rows = pl.ds(8 * index, 8)
        inside = index in (1, 14)
        x, y, k = (ext[field, rows] if inside else zeros for field in range(3))
        f = ext[3, rows].astype(jnp.int32) if inside else no_flags
        store_moved(0, rows, (x, zeros), (y, zeros))
        if index in (0, 15):
            for buffer_step in range(4):
                for tile in range(2):
                    pos[1, 0, buffer_step, tile, rows] = zeros
                    pos[1, 1, buffer_step, tile, rows] = zeros
        else:
            store_moved(1, rows, (x, zeros), (y, zeros))
        for step in range(4):
            stiff[step, 0, rows], stiff[step, 1, rows] = ahead(k, zeros, step)
        for step in range(3):
            flags[step, 0, rows], flags[step, 1, rows] = ahead(f, no_flags, step)

    lax.fori_loop(2, 14, set_up, 0)

    def set_coefs(index, carry):
        start = pl.multiple_of(8 * index, 8)
        rows = pl.ds(start, 8)
        for tile in range(2):
            itself = stiff[0, tile, rows]
            bits = flags[0, tile, rows]
            for j, (row_step, col_step, bit, far) in enumerate(BONDS):
                there = pl.ds(start + row_step, 8)
                word = flags[col_step, tile, there] if far else bits
                value = (0.5 * TIME_STEP) * (itself + stiff[col_step, tile, there])
                coef[j, tile, rows] = jnp.where((word & (1 << bit)) != 0, value, 0.0)
        return carry

    lax.fori_loop(1, 15, set_coefs, 0)

    CH = 16

    def forces(buffer, start):
        rows = pl.ds(start, CH)
        for tile in range(2):
            x, y = pos[buffer, 0, 0, tile, rows], pos[buffer, 1, 0, tile, rows]
            from_row = {row_step: x - float(row_step) if row_step else x for row_step in range(-2, 4)}
            sum_x = sum_y = None
            for j, (row_step, col_step, _, _) in enumerate(BONDS):
                there = pl.ds(start + row_step, CH)
                dx = pos[buffer, 0, col_step, tile, there] - from_row[row_step]
                dy = pos[buffer, 1, col_step, tile, there] - y
                square = jnp.maximum(dx * dx + dy * dy, TINY)
                inverse_length = 1.0 / math.sqrt(row_step * row_step + col_step * col_step)
                weight = coef[j, tile, rows] * (inverse_length - lax.rsqrt(square))
                fx, fy = weight * dx, weight * dy
                pair[j, 0, tile, rows] = fx
                pair[j, 1, tile, rows] = fy
                sum_x = fx if sum_x is None else sum_x + fx
                sum_y = fy if sum_y is None else sum_y + fy
            near_sum[0, tile, rows] = sum_x
            near_sum[1, tile, rows] = sum_y

    def move(buffer, scale, start):
        rows = pl.ds(start, CH)
        new = []
        for component in range(2):
            total = [near_sum[component, 0, rows], near_sum[component, 1, rows]]
            for col_step in range(4):
                sums = []
                for tile in range(2):
                    part = None
                    for j, (row_step, step, _, _) in enumerate(BONDS):
                        if step == col_step:
                            value = pair[j, component, tile, pl.ds(start - row_step, CH)]
                            part = value if part is None else part + value
                    sums.append(part)
                back = behind(sums[0], sums[1], col_step)
                total = [total[0] - back[0], total[1] - back[1]]
            moved = []
            for tile in range(2):
                speed = half[component, tile, rows] + scale * (total[tile] + push[component, tile, rows])
                half[component, tile, rows] = speed
                moved.append(pos[buffer, component, 0, tile, rows] + TIME_STEP * speed)
            new.append(moved)
        store_moved(1 - buffer, rows, new[0], new[1])

    def advance(k, carry):
        buffer = lax.rem(k, 2)
        scale = jnp.where((k == 0) | (k == STEPS), 0.5, 1.0).astype(jnp.float32)
        first, last = (15 + 3 * k) // 8, (111 - 3 * k) // 8 + 1
        count = (last - first + 1) // 2

        def force_chunk(i, c):
            forces(buffer, pl.multiple_of(8 * (first + 2 * i), 8))
            return c

        lax.fori_loop(0, count, force_chunk, 0)
        first, last = (18 + 3 * k) // 8, (109 - 3 * k) // 8 + 1
        count = (last - first + 1) // 2

        def move_chunk(i, c):
            move(buffer, scale, pl.multiple_of(8 * (first + 2 * i), 8))
            return c

        lax.fori_loop(0, count, move_chunk, 0)
        return carry

    lax.fori_loop(0, STEPS + 1, advance, 0)
    own = pl.ds(BASE, ROWS)
    for component in range(2):
        disp_out[component] = pos[STEPS % 2, component, 0, 0, own]
        vel_out[component] = half[component, 0, own]


def run_steps(ext, left, right):
    vmem = pl.BlockSpec(memory_space=pltpu.VMEM)
    out = jax.ShapeDtypeStruct((2, ROWS, COLS), jnp.float32)
    return pl.pallas_call(
        steps_kernel,
        out_shape=(out, out),
        in_specs=[vmem] * 3,
        out_specs=(vmem, vmem),
        scratch_shapes=[
            pltpu.VMEM((2, 2, 4, 2, TALL, COLS), jnp.float32),
            pltpu.VMEM((2, 2, TALL, COLS), jnp.float32),
            pltpu.VMEM((2, 2, TALL, COLS), jnp.float32),
            pltpu.VMEM((14, 2, TALL, COLS), jnp.float32),
            pltpu.VMEM((14, 2, 2, TALL, COLS), jnp.float32),
            pltpu.VMEM((2, 2, TALL, COLS), jnp.float32),
            pltpu.VMEM((4, 2, TALL, COLS), jnp.float32),
            pltpu.VMEM((3, 2, TALL, COLS), jnp.int32),
        ],
        compiler_params=pltpu.CompilerParams(vmem_limit_bytes=32 * 1024 * 1024),
        name="steps",
    )(*(pltpu.with_memory_space_constraint(a, pltpu.VMEM) for a in (ext, left, right)))


def solution(mesh):
    shape_x, shape_y = mesh.shape["gx"], mesh.shape["gy"]

    def on_device(disp, vel, stiffness, body_force, bond_bits):
        halos = exchange(shape_x, shape_y, disp, vel, stiffness, body_force, bond_bits)
        return run_steps(*halos)

    plane, word = P("gx", "gy"), P(None, "gx", "gy")
    return jax.shard_map(
        on_device, mesh=mesh, in_specs=(word, word, plane, word, word), out_specs=(word, word), check_vma=False
    )
```

```python
import functools
import math

import jax
import jax.numpy as jnp
from jax import lax
from jax.experimental import pallas as pl
from jax.experimental.pallas import tpu as pltpu
from jax.sharding import PartitionSpec as P

STEPS = 10
TIME_STEP = 0.04
ROWS = 32
COLS = 128
BASE = 48
TALL = 128
SIDE = 96
TINY = 1.2e-38
MESH = pl.DeviceIdType.MESH
OWN = pl.ds(BASE, ROWS)
GROUPS = [0, 32, 64, 96]


def upper_shell():
    upper = []
    for row_step in range(0, 4):
        for col_step in range(-3, 4):
            if row_step * row_step + col_step * col_step <= 9 and (row_step > 0 or col_step > 0):
                upper.append((row_step, col_step))
    return upper


def half_shell():
    bonds = []
    for index, (row_step, col_step) in enumerate(upper_shell()):
        if col_step >= 0:
            bonds.append((row_step, col_step, index, False))
        else:
            bonds.append((-row_step, -col_step, index, True))
    return sorted(bonds, key=lambda bond: (bond[1], bond[0]))


BONDS = half_shell()


def lanes_of(shape):
    return lax.broadcasted_iota(jnp.int32, shape, len(shape) - 1)


def ahead(first, second, step):
    inside = lanes_of(first.shape) < COLS - step
    a, b = pltpu.roll(first, COLS - step, 1), pltpu.roll(second, COLS - step, 1)
    return jnp.where(inside, a, b), jnp.where(inside, b, a)


def behind(first, second, step):
    if step == 0:
        return first, second
    inside = lanes_of(first.shape) >= step
    a, b = pltpu.roll(first, step, 1), pltpu.roll(second, step, 1)
    return jnp.where(inside, a, b), jnp.where(inside, b, a)


def spread(pos, start, chunk):
    rows = pl.ds(start, chunk)
    for component in range(2):
        first, second = pos[component, 0, 0, rows], pos[component, 0, 1, rows]
        for step in range(1, 4):
            a, b = ahead(first, second, step)
            pos[component, step, 0, rows] = a + float(step) if component else a
            pos[component, step, 1, rows] = b + float(step) if component else b


def forces(pos, coef, pair, near_sum, start, chunk):
    rows = pl.ds(start, chunk)
    for tile in range(2):
        x, y = pos[0, 0, tile, rows], pos[1, 0, tile, rows]
        from_row = {row_step: x - float(row_step) if row_step else x for row_step in range(-2, 4)}
        sum_x = sum_y = None
        for j, (row_step, col_step, _, _) in enumerate(BONDS):
            there = pl.ds(start + row_step, chunk)
            dx = pos[0, col_step, tile, there] - from_row[row_step]
            dy = pos[1, col_step, tile, there] - y
            square = jnp.maximum(dx * dx + dy * dy, TINY)
            inverse_length = 1.0 / math.sqrt(row_step * row_step + col_step * col_step)
            weight = coef[j, tile, rows] * (inverse_length - lax.rsqrt(square))
            fx, fy = weight * dx, weight * dy
            pair[j, 0, tile, rows] = fx
            pair[j, 1, tile, rows] = fy
            sum_x = fx if sum_x is None else sum_x + fx
            sum_y = fy if sum_y is None else sum_y + fy
        near_sum[0, tile, rows] = sum_x
        near_sum[1, tile, rows] = sum_y


def force_loop(k, pos, coef, pair, near_sum):
    first, last = (15 + 3 * k) // 8, (111 - 3 * k) // 8 + 1

    def force_chunk(i, carry):
        forces(pos, coef, pair, near_sum, pl.multiple_of(8 * (first + 2 * i), 8), 16)
        return carry

    lax.fori_loop(0, (last - first + 1) // 2, force_chunk, 0)


def move(pos, pair, near_sum, push, half, scale, start, chunk):
    rows = pl.ds(start, chunk)
    for component in range(2):
        total = [near_sum[component, 0, rows], near_sum[component, 1, rows]]
        for col_step in range(4):
            sums = []
            for tile in range(2):
                part = None
                for j, (row_step, step, _, _) in enumerate(BONDS):
                    if step == col_step:
                        value = pair[j, component, tile, pl.ds(start - row_step, chunk)]
                        part = value if part is None else part + value
                sums.append(part)
            back = behind(sums[0], sums[1], col_step)
            total = [total[0] - back[0], total[1] - back[1]]
        for tile in range(2):
            speed = half[component, tile, rows] + scale * (total[tile] + push[component, tile, rows])
            half[component, tile, rows] = speed
            pos[component, 0, tile, rows] = pos[component, 0, tile, rows] + TIME_STEP * speed


def packed(fields, start):
    lanes = lanes_of((ROWS, COLS))
    total = None
    for field, group in zip(fields, GROUPS, strict=True):
        moved = pltpu.roll(field, (group - start) % COLS, 1)
        total = moved if total is None else jnp.where((lanes >= group) & (lanes < group + 32), moved, total)
    return total


def beside(right, left, word, group, rows):
    from_right = pltpu.roll(right[word, rows], (-32 * group) % COLS, 1)
    from_left = pltpu.roll(left[word, rows], (96 - 32 * group) % COLS, 1)
    return from_right, from_left


def set_up(near, left, right, pos, coef, stiff, flags):
    lanes8 = lanes_of((8, COLS))
    zeros = jnp.zeros((8, COLS), jnp.float32)
    for index in range(1, 15):
        rows = pl.ds(8 * index, 8)
        x, y, k, bits = (near[field, rows] for field in range(4))
        pos[0, 0, 0, rows] = x
        pos[1, 0, 0, rows] = y
        stiff[0, 0, rows] = k
        flags[0, 0, rows] = bits.astype(jnp.int32)
        others = [zeros] * 4
        if 2 <= index < 14:
            side = pl.ds(8 * index - 16, 8)
            for field in range(4):
                from_right, from_left = beside(right, left, 0, field, side)
                value = jnp.where(lanes8 < 32, from_right, jnp.where(lanes8 >= 96, from_left, 0.0))
                if 6 <= index < 10:
                    far_right = pltpu.roll(right[1, side], (32 - (32 * field + 30)) % COLS, 1)
                    far_left = pltpu.roll(left[1, side], (95 - (32 * field + 1)) % COLS, 1)
                    value = jnp.where(lanes8 == 32, far_right, jnp.where(lanes8 == 95, far_left, value))
                others[field] = value
        pos[0, 0, 1, rows] = others[0]
        pos[1, 0, 1, rows] = others[1]
        stiff[0, 1, rows] = others[2]
        flags[0, 1, rows] = others[3].astype(jnp.int32)
    for index in range(1, 15):
        rows = pl.ds(8 * index, 8)
        for step in range(1, 4):
            stiff[step, 0, rows], stiff[step, 1, rows] = ahead(stiff[0, 0, rows], stiff[0, 1, rows], step)
        for step in range(1, 3):
            flags[step, 0, rows], flags[step, 1, rows] = ahead(flags[0, 0, rows], flags[0, 1, rows], step)
        spread(pos, 8 * index, 8)

    def set_coefs(index, carry):
        start = pl.multiple_of(8 * index, 8)
        rows = pl.ds(start, 8)
        for tile in range(2):
            itself = stiff[0, tile, rows]
            bits = flags[0, tile, rows]
            for j, (row_step, col_step, bit, far) in enumerate(BONDS):
                there = pl.ds(start + row_step, 8)
                word = flags[col_step, tile, there] if far else bits
                value = 0.5 * (itself + stiff[col_step, tile, there])
                coef[j, tile, rows] = jnp.where((word & (1 << bit)) != 0, value, 0.0)
        return carry

    lax.fori_loop(1, 15, set_coefs, 0)


def exchange_kernel(shape_x, shape_y, disp, vel, stiff_own, body, bits, half, push, pos, coef, pair, near_sum,
                    near, left, right, stiff, flags, bits_own, to_west, to_east, local_sem, send_sem, recv_sem):
    gx, gy = lax.axis_index("gx"), lax.axis_index("gy")

    def neighbour(row_step, col_step):
        return (
            lax.rem(gx + row_step + shape_x, shape_x),
            lax.rem(gy + col_step + shape_y, shape_y),
        )

    around = [(-1, 0), (1, 0), (0, -1), (0, 1), (-1, -1), (-1, 1), (1, -1), (1, 1), (-2, 0), (2, 0)]
    barrier = pltpu.get_barrier_semaphore()
    for step in around:
        pl.semaphore_signal(barrier, inc=1, device_id=neighbour(*step), device_id_type=MESH)

    local = [
        pltpu.make_async_copy(bits.at[0], bits_own, local_sem.at[0]),
        pltpu.make_async_copy(disp, near.at[pl.ds(0, 2), OWN], local_sem.at[1]),
        pltpu.make_async_copy(stiff_own, near.at[2, OWN], local_sem.at[2]),
        pltpu.make_async_copy(vel, half.at[:, 0, OWN], local_sem.at[3]),
        pltpu.make_async_copy(body, push.at[:, 0, OWN], local_sem.at[4]),
    ]
    for copy in local:
        copy.start()
    zeros = jnp.zeros((8, COLS), jnp.float32)
    for index in (0, 15):
        rows = pl.ds(8 * index, 8)
        for step in range(4):
            for tile in range(2):
                pos[0, step, tile, rows] = zeros
                pos[1, step, tile, rows] = zeros
                stiff[step, tile, rows] = zeros
        for step in range(3):
            for tile in range(2):
                flags[step, tile, rows] = jnp.zeros((8, COLS), jnp.int32)
    for copy in local:
        copy.wait()
    near[3, OWN] = bits_own[...].astype(jnp.float32)

    first_four = [near[field, OWN] for field in range(4)]
    last_four = [half[0, 0, OWN], half[1, 0, OWN], push[0, 0, OWN], push[1, 0, OWN]]
    lanes = lanes_of((ROWS, COLS))
    to_west[0] = packed(first_four, 0)
    to_east[0] = packed(first_four, 96)
    west, east = packed(last_four, 0), packed(last_four, 96)
    for field in range(4):
        group = GROUPS[field]
        west = jnp.where(lanes == group + 30, pltpu.roll(first_four[field], (group + 30 - 32) % COLS, 1), west)
        east = jnp.where(lanes == group + 1, pltpu.roll(first_four[field], (group + 1 - 95) % COLS, 1), east)
    to_west[1] = west
    to_east[1] = east

    pl.semaphore_wait(barrier, len(around))

    four = pl.ds(0, 4)
    plan = [
        (near.at[four, OWN], near.at[four, pl.ds(BASE + ROWS, ROWS)], (-1, 0)),
        (near.at[four, OWN], near.at[four, pl.ds(BASE - ROWS, ROWS)], (1, 0)),
        (to_west, right.at[:, pl.ds(64, 32)], (-1, -1)),
        (to_east, left.at[:, pl.ds(64, 32)], (-1, 1)),
        (to_west, right.at[:, pl.ds(0, 32)], (1, -1)),
        (to_east, left.at[:, pl.ds(0, 32)], (1, 1)),
        (to_west, right.at[:, pl.ds(32, 32)], (0, -1)),
        (to_east, left.at[:, pl.ds(32, 32)], (0, 1)),
        (near.at[four, pl.ds(BASE, 8)], near.at[four, pl.ds(BASE + 64, 8)], (-2, 0)),
        (near.at[four, pl.ds(BASE + 24, 8)], near.at[four, pl.ds(BASE - 40, 8)], (2, 0)),
        (half.at[:, 0, OWN], half.at[:, 0, pl.ds(BASE + ROWS, ROWS)], (-1, 0)),
        (half.at[:, 0, OWN], half.at[:, 0, pl.ds(BASE - ROWS, ROWS)], (1, 0)),
        (push.at[:, 0, OWN], push.at[:, 0, pl.ds(BASE + ROWS, ROWS)], (-1, 0)),
        (push.at[:, 0, OWN], push.at[:, 0, pl.ds(BASE - ROWS, ROWS)], (1, 0)),
    ]
    copies = [
        pltpu.make_async_remote_copy(
            src_ref=source,
            dst_ref=target,
            send_sem=send_sem.at[index],
            recv_sem=recv_sem.at[index],
            device_id=neighbour(*step),
            device_id_type=MESH,
        )
        for index, (source, target, step) in enumerate(plan)
    ]
    order = [2, 3, 4, 5, 0, 1, 6, 7, 8, 9]
    for index in order:
        copies[index].start()
    for index in (0, 1):
        copies[index].wait_send()
    for copy in copies[10:]:
        copy.start()
    for copy in copies[:10]:
        copy.wait_recv()
    set_up(near, left, right, pos, coef, stiff, flags)
    force_loop(0, pos, coef, pair, near_sum)
    lanes8 = lanes_of((8, COLS))
    for index in range(2, 14):
        rows = pl.ds(8 * index, 8)
        side = pl.ds(8 * index - 16, 8)
        for field in range(4):
            from_right, from_left = beside(right, left, 1, field, side)
            value = jnp.where(lanes8 < 30, from_right, jnp.where(lanes8 >= 98, from_left, 0.0))
            (half if field < 2 else push)[field % 2, 1, rows] = value
    for copy in copies[10:]:
        copy.wait_recv()
    for copy in copies[2:]:
        copy.wait_send()


F32 = jnp.float32
POS = (2, 4, 2, TALL, COLS)
PAIR = (14, 2, 2, TALL, COLS)
SUM = (2, 2, TALL, COLS)


def exchange(shape_x, shape_y, *args):
    hbm = pl.BlockSpec(memory_space=pltpu.HBM)
    vmem = pl.BlockSpec(memory_space=pltpu.VMEM)
    shapes = (SUM, SUM, POS, (14, 2, TALL, COLS), PAIR, SUM)
    return pl.pallas_call(
        functools.partial(exchange_kernel, shape_x, shape_y),
        out_shape=tuple(pltpu.VMEM(shape, F32) for shape in shapes),
        in_specs=[hbm] * 5,
        out_specs=(vmem,) * len(shapes),
        scratch_shapes=[
            pltpu.VMEM((4, TALL, COLS), F32),
            pltpu.VMEM((2, SIDE, COLS), F32),
            pltpu.VMEM((2, SIDE, COLS), F32),
            pltpu.VMEM((4, 2, TALL, COLS), F32),
            pltpu.VMEM((3, 2, TALL, COLS), jnp.int32),
            pltpu.VMEM((ROWS, COLS), jnp.int32),
            pltpu.VMEM((2, ROWS, COLS), F32),
            pltpu.VMEM((2, ROWS, COLS), F32),
            pltpu.SemaphoreType.DMA((5,)),
            pltpu.SemaphoreType.DMA((14,)),
            pltpu.SemaphoreType.DMA((14,)),
        ],
        compiler_params=pltpu.CompilerParams(
            collective_id=0, has_side_effects=True, vmem_limit_bytes=24 * 1024 * 1024
        ),
        name="exchange",
    )(*(pltpu.with_memory_space_constraint(a, pltpu.HBM) for a in args))


def region(k):
    return (18 + 3 * k) // 8, (109 - 3 * k) // 8 + 1


def steps_kernel(push, coef, half_in, pos_in, pair_in, sum_in, disp_out, vel_out, half, pos, pair, near_sum):
    del half_in, pos_in, pair_in, sum_in
    k = 0
    while k < STEPS:
        first, last = region(k)
        end = k + 1
        while end < STEPS and region(end) == (first, last):
            end += 1

        def advance(step, carry, starting=k == 0, first=first, last=last):
            scale = jnp.where(step == 0, 0.5 * TIME_STEP, TIME_STEP).astype(F32) if starting else TIME_STEP
            for index in range(first, last, 2):
                move(pos, pair, near_sum, push, half, scale, 8 * index, 16)
            for index in range(first, last, 2):
                spread(pos, 8 * index, 16)
            for index in range(first, last, 2):
                forces(pos, coef, pair, near_sum, 8 * index, 16)
            return carry

        lax.fori_loop(k, end, advance, 0)
        k = end
    for component in range(2):
        disp_out[component] = pos[component, 0, 0, OWN]
    first, last = region(STEPS)
    for index in range(first, last, 2):
        move(pos, pair, near_sum, push, half, 0.5 * TIME_STEP, 8 * index, 16)
    for component in range(2):
        vel_out[component] = half[component, 0, OWN]


def run_steps(half, push, pos, coef, pair, near_sum):
    vmem = pl.BlockSpec(memory_space=pltpu.VMEM)
    out = jax.ShapeDtypeStruct((2, ROWS, COLS), F32)
    arrays = (push, coef, half, pos, pair, near_sum)
    return pl.pallas_call(
        steps_kernel,
        out_shape=(out, out, *(pltpu.VMEM(shape, F32) for shape in (SUM, POS, PAIR, SUM))),
        in_specs=[vmem] * len(arrays),
        out_specs=(vmem,) * 6,
        input_output_aliases={2: 2, 3: 3, 4: 4, 5: 5},
        compiler_params=pltpu.CompilerParams(vmem_limit_bytes=24 * 1024 * 1024),
        name="steps",
    )(*(pltpu.with_memory_space_constraint(a, pltpu.VMEM) for a in arrays))[:2]


def solution(mesh):
    shape_x, shape_y = mesh.shape["gx"], mesh.shape["gy"]

    def on_device(disp, vel, stiffness, body_force, bond_bits):
        started = exchange(shape_x, shape_y, disp, vel, stiffness, body_force, bond_bits)
        return run_steps(*started)

    plane, word = P("gx", "gy"), P(None, "gx", "gy")
    return jax.shard_map(
        on_device, mesh=mesh, in_specs=(word, word, plane, word, word), out_specs=(word, word), check_vma=False
    )
```

```python
import functools
import math

import jax
import jax.numpy as jnp
from jax import lax
from jax.experimental import pallas as pl
from jax.experimental.pallas import tpu as pltpu
from jax.sharding import PartitionSpec as P

STEPS = 10
TIME_STEP = 0.04
ROWS = 32
COLS = 128
BASE = 48
TALL = 128
SIDE = 96
TINY = 1.2e-38
MESH = pl.DeviceIdType.MESH
OWN = pl.ds(BASE, ROWS)
WEST = [0, 32, 64, 96]
EAST = [96, 0, 32, 64]


def upper_shell():
    upper = []
    for row_step in range(0, 4):
        for col_step in range(-3, 4):
            if row_step * row_step + col_step * col_step <= 9 and (row_step > 0 or col_step > 0):
                upper.append((row_step, col_step))
    return upper


def half_shell():
    bonds = []
    for index, (row_step, col_step) in enumerate(upper_shell()):
        if col_step >= 0:
            bonds.append((row_step, col_step, index, False))
        else:
            bonds.append((-row_step, -col_step, index, True))
    return sorted(bonds, key=lambda bond: (bond[1], bond[0]))


BONDS = half_shell()


def lanes_of(shape):
    return lax.broadcasted_iota(jnp.int32, shape, len(shape) - 1)


def ahead(first, second, step):
    inside = lanes_of(first.shape) < COLS - step
    a, b = pltpu.roll(first, COLS - step, 1), pltpu.roll(second, COLS - step, 1)
    return jnp.where(inside, a, b), jnp.where(inside, b, a)


def behind(first, second, step):
    if step == 0:
        return first, second
    inside = lanes_of(first.shape) >= step
    a, b = pltpu.roll(first, step, 1), pltpu.roll(second, step, 1)
    return jnp.where(inside, a, b), jnp.where(inside, b, a)


def spread(pos, start, chunk):
    rows = pl.ds(start, chunk)
    for component in range(2):
        first, second = pos[component, 0, 0, rows], pos[component, 0, 1, rows]
        for step in range(1, 4):
            a, b = ahead(first, second, step)
            pos[component, step, 0, rows] = a + float(step) if component else a
            pos[component, step, 1, rows] = b + float(step) if component else b


def forces(pos, coef, pair, near_sum, start, chunk):
    rows = pl.ds(start, chunk)
    for tile in range(2):
        x, y = pos[0, 0, tile, rows], pos[1, 0, tile, rows]
        from_row = {row_step: x - float(row_step) if row_step else x for row_step in range(-2, 4)}
        sum_x = sum_y = None
        for j, (row_step, col_step, _, _) in enumerate(BONDS):
            there = pl.ds(start + row_step, chunk)
            dx = pos[0, col_step, tile, there] - from_row[row_step]
            dy = pos[1, col_step, tile, there] - y
            square = jnp.maximum(dx * dx + dy * dy, TINY)
            inverse_length = 1.0 / math.sqrt(row_step * row_step + col_step * col_step)
            weight = coef[j, tile, rows] * (inverse_length - lax.rsqrt(square))
            fx, fy = weight * dx, weight * dy
            pair[j, 0, tile, rows] = fx
            pair[j, 1, tile, rows] = fy
            sum_x = fx if sum_x is None else sum_x + fx
            sum_y = fy if sum_y is None else sum_y + fy
        near_sum[0, tile, rows] = sum_x
        near_sum[1, tile, rows] = sum_y


def force_loop(k, pos, coef, pair, near_sum):
    first, last = (15 + 3 * k) // 8, (111 - 3 * k) // 8 + 1

    def force_chunk(i, carry):
        forces(pos, coef, pair, near_sum, pl.multiple_of(8 * (first + 2 * i), 8), 16)
        return carry

    lax.fori_loop(0, (last - first + 1) // 2, force_chunk, 0)


def move(pos, pair, near_sum, flow, scale, start, chunk, last=False):
    rows = pl.ds(start, chunk)
    for component in range(2):
        total = [near_sum[component, 0, rows], near_sum[component, 1, rows]]
        for col_step in range(4):
            sums = []
            for tile in range(2):
                part = None
                for j, (row_step, step, _, _) in enumerate(BONDS):
                    if step == col_step:
                        value = pair[j, component, tile, pl.ds(start - row_step, chunk)]
                        part = value if part is None else part + value
                sums.append(part)
            back = behind(sums[0], sums[1], col_step)
            total = [total[0] - back[0], total[1] - back[1]]
        for tile in range(1 if last else 2):
            speed = flow[component, tile, rows] + scale * (total[tile] + flow[2 + component, tile, rows])
            flow[component, tile, rows] = speed
            if not last:
                pos[component, 0, tile, rows] = pos[component, 0, tile, rows] + TIME_STEP * speed


def packed(fields, start, groups):
    lanes = lanes_of((ROWS, COLS))
    total = None
    for field, group in zip(fields, groups, strict=True):
        moved = pltpu.roll(field, (group - start) % COLS, 1) if group != start else field
        total = moved if total is None else jnp.where((lanes >= group) & (lanes < group + 32), moved, total)
    return total


def beside(right, left, word, field, rows):
    lanes = lanes_of((8, COLS))
    at_right, at_left = WEST[field], EAST[field]
    value = jnp.where((lanes >= at_left) & (lanes < at_left + 32), left[word, rows], 0.0)
    value = jnp.where((lanes >= at_right) & (lanes < at_right + 32), right[word, rows], value)
    return pltpu.roll(value, -at_right % COLS, 1) if at_right else value


def begin(near, pos, stiff, flags, tiles):
    for index in tiles:
        rows = pl.ds(8 * index, 8)
        x, y, k = (near[field, rows] for field in range(3))
        bits = near[3, rows].astype(jnp.int32)
        pos[0, 0, 0, rows] = x
        pos[1, 0, 0, rows] = y
        stiff[0, 0, rows] = k
        flags[0, 0, rows] = bits
        for step in range(1, 4):
            pos[0, step, 0, rows] = pltpu.roll(x, COLS - step, 1)
            pos[1, step, 0, rows] = pltpu.roll(y, COLS - step, 1)
            stiff[step, 0, rows] = pltpu.roll(k, COLS - step, 1)
        for step in range(1, 3):
            flags[step, 0, rows] = pltpu.roll(bits, COLS - step, 1)


def finish(left, right, pos, coef, stiff, flags):
    lanes8 = lanes_of((8, COLS))
    zeros = jnp.zeros((8, COLS), jnp.float32)
    for index in range(1, 15):
        rows = pl.ds(8 * index, 8)
        others = [zeros] * 4
        if 2 <= index < 14:
            side = pl.ds(8 * index - 16, 8)
            for field in range(4):
                value = beside(right, left, 0, field, side)
                if 6 <= index < 10:
                    far_right = pltpu.roll(right[1, side], (32 - (WEST[field] + 30)) % COLS, 1)
                    far_left = pltpu.roll(left[1, side], (95 - (EAST[field] + 1)) % COLS, 1)
                    value = jnp.where(lanes8 == 32, far_right, jnp.where(lanes8 == 95, far_left, value))
                others[field] = value
        pos[0, 0, 1, rows] = others[0]
        pos[1, 0, 1, rows] = others[1]
        stiff[0, 1, rows] = others[2]
        flags[0, 1, rows] = others[3].astype(jnp.int32)

    def complete(ref, where, step, rows, bias):
        inside = lanes8 < COLS - step
        own, other = ref[(*where, step, 0, rows)], pltpu.roll(ref[(*where, 0, 1, rows)], COLS - step, 1)
        first, second = jnp.where(inside, own, other), jnp.where(inside, other, own)
        ref[(*where, step, 0, rows)] = first + bias if bias else first
        ref[(*where, step, 1, rows)] = second + bias if bias else second

    for index in range(1, 15):
        rows = pl.ds(8 * index, 8)
        for step in range(1, 4):
            complete(pos, (0,), step, rows, 0.0)
            complete(pos, (1,), step, rows, float(step))
            complete(stiff, (), step, rows, 0.0)
        for step in range(1, 3):
            complete(flags, (), step, rows, 0)

    def set_coefs(index, carry):
        start = pl.multiple_of(8 * index, 8)
        rows = pl.ds(start, 8)
        for tile in range(2):
            itself = stiff[0, tile, rows]
            bits = flags[0, tile, rows]
            for j, (row_step, col_step, bit, far) in enumerate(BONDS):
                there = pl.ds(start + row_step, 8)
                word = flags[col_step, tile, there] if far else bits
                value = 0.5 * (itself + stiff[col_step, tile, there])
                coef[j, tile, rows] = jnp.where((word & (1 << bit)) != 0, value, 0.0)
        return carry

    lax.fori_loop(1, 15, set_coefs, 0)


def exchange_kernel(shape_x, shape_y, disp, vel, stiff_own, body, bits, flow, pos, coef, pair, near_sum,
                    near, left, right, stiff, flags, bits_own, to_west, to_east, local_sem, send_sem, recv_sem):
    gx, gy = lax.axis_index("gx"), lax.axis_index("gy")

    def neighbour(row_step, col_step):
        return (
            lax.rem(gx + row_step + shape_x, shape_x),
            lax.rem(gy + col_step + shape_y, shape_y),
        )

    around = [(-1, -1), (-1, 1), (1, -1), (1, 1), (-1, 0), (1, 0), (0, -1), (0, 1), (-2, 0), (2, 0)]
    barrier = pltpu.get_barrier_semaphore()
    for step in around:
        pl.semaphore_signal(barrier, inc=1, device_id=neighbour(*step), device_id_type=MESH)

    local = [
        pltpu.make_async_copy(bits.at[0], bits_own, local_sem.at[0]),
        pltpu.make_async_copy(disp, near.at[pl.ds(0, 2), OWN], local_sem.at[1]),
        pltpu.make_async_copy(stiff_own, near.at[2, OWN], local_sem.at[2]),
        pltpu.make_async_copy(vel, flow.at[pl.ds(0, 2), 0, OWN], local_sem.at[3]),
        pltpu.make_async_copy(body, flow.at[pl.ds(2, 2), 0, OWN], local_sem.at[4]),
    ]
    for copy in local:
        copy.start()
    zeros = jnp.zeros((8, COLS), jnp.float32)
    for index in (0, 15):
        rows = pl.ds(8 * index, 8)
        for step in range(4):
            for tile in range(2):
                pos[0, step, tile, rows] = zeros
                pos[1, step, tile, rows] = zeros
                stiff[step, tile, rows] = zeros
        for step in range(3):
            for tile in range(2):
                flags[step, tile, rows] = jnp.zeros((8, COLS), jnp.int32)
    for copy in local:
        copy.wait()
    near[3, OWN] = bits_own[...].astype(jnp.float32)

    first_four = [near[field, OWN] for field in range(4)]
    last_four = [flow[field, 0, OWN] for field in range(4)]
    lanes = lanes_of((ROWS, COLS))
    to_west[0] = packed(first_four, 0, WEST)
    to_east[0] = packed(first_four, 96, EAST)
    west, east = packed(last_four, 0, WEST), packed(last_four, 96, EAST)
    for field in range(4):
        at_west, at_east = WEST[field] + 30, EAST[field] + 1
        west = jnp.where(lanes == at_west, pltpu.roll(first_four[field], (at_west - 32) % COLS, 1), west)
        east = jnp.where(lanes == at_east, pltpu.roll(first_four[field], (at_east - 95) % COLS, 1), east)
    to_west[1] = west
    to_east[1] = east
    begin(near, pos, stiff, flags, range(6, 10))

    pl.semaphore_wait(barrier, len(around))

    four = pl.ds(0, 4)
    plan = [
        (near.at[four, OWN], near.at[four, pl.ds(BASE + ROWS, ROWS)], (-1, 0)),
        (near.at[four, OWN], near.at[four, pl.ds(BASE - ROWS, ROWS)], (1, 0)),
        (to_west.at[0], right.at[0, pl.ds(64, 32)], (-1, -1)),
        (to_east.at[0], left.at[0, pl.ds(64, 32)], (-1, 1)),
        (to_west.at[0], right.at[0, pl.ds(0, 32)], (1, -1)),
        (to_east.at[0], left.at[0, pl.ds(0, 32)], (1, 1)),
        (to_west, right.at[:, pl.ds(32, 32)], (0, -1)),
        (to_east, left.at[:, pl.ds(32, 32)], (0, 1)),
        (near.at[four, pl.ds(BASE, 8)], near.at[four, pl.ds(BASE + 64, 8)], (-2, 0)),
        (near.at[four, pl.ds(BASE + 24, 8)], near.at[four, pl.ds(BASE - 40, 8)], (2, 0)),
        (to_west.at[1], right.at[1, pl.ds(64, 32)], (-1, -1)),
        (to_east.at[1], left.at[1, pl.ds(64, 32)], (-1, 1)),
        (to_west.at[1], right.at[1, pl.ds(0, 32)], (1, -1)),
        (to_east.at[1], left.at[1, pl.ds(0, 32)], (1, 1)),
        (flow.at[:, 0, OWN], flow.at[:, 0, pl.ds(BASE + ROWS, ROWS)], (-1, 0)),
        (flow.at[:, 0, OWN], flow.at[:, 0, pl.ds(BASE - ROWS, ROWS)], (1, 0)),
    ]
    copies = [
        pltpu.make_async_remote_copy(
            src_ref=source,
            dst_ref=target,
            send_sem=send_sem.at[index],
            recv_sem=recv_sem.at[index],
            device_id=neighbour(*step),
            device_id_type=MESH,
        )
        for index, (source, target, step) in enumerate(plan)
    ]
    order = [2, 3, 4, 5, 0, 1, 6, 7, 8, 9, 10, 11, 12, 13]
    for index in order:
        copies[index].start()
    for index in (0, 1):
        copies[index].wait_send()
    for copy in copies[14:]:
        copy.start()
    for index in (0, 1, 8, 9):
        copies[index].wait_recv()
    begin(near, pos, stiff, flags, [*range(1, 6), *range(10, 15)])
    for copy in copies[2:8]:
        copy.wait_recv()
    finish(left, right, pos, coef, stiff, flags)
    force_loop(0, pos, coef, pair, near_sum)
    for copy in copies[10:14]:
        copy.wait_recv()
    lanes8 = lanes_of((8, COLS))
    for index in range(2, 14):
        rows = pl.ds(8 * index, 8)
        side = pl.ds(8 * index - 16, 8)
        for field in range(4):
            value = beside(right, left, 1, field, side)
            flow[field, 1, rows] = jnp.where((lanes8 < 30) | (lanes8 >= 98), value, 0.0)
    for copy in copies[14:]:
        copy.wait_recv()
    for copy in copies[2:]:
        copy.wait_send()


F32 = jnp.float32
POS = (2, 4, 2, TALL, COLS)
PAIR = (14, 2, 2, TALL, COLS)
SUM = (2, 2, TALL, COLS)
FLOW = (4, 2, TALL, COLS)


def exchange(shape_x, shape_y, *args):
    hbm = pl.BlockSpec(memory_space=pltpu.HBM)
    vmem = pl.BlockSpec(memory_space=pltpu.VMEM)
    shapes = (FLOW, POS, (14, 2, TALL, COLS), PAIR, SUM)
    return pl.pallas_call(
        functools.partial(exchange_kernel, shape_x, shape_y),
        out_shape=tuple(pltpu.VMEM(shape, F32) for shape in shapes),
        in_specs=[hbm] * 5,
        out_specs=(vmem,) * len(shapes),
        scratch_shapes=[
            pltpu.VMEM((4, TALL, COLS), F32),
            pltpu.VMEM((2, SIDE, COLS), F32),
            pltpu.VMEM((2, SIDE, COLS), F32),
            pltpu.VMEM((4, 2, TALL, COLS), F32),
            pltpu.VMEM((3, 2, TALL, COLS), jnp.int32),
            pltpu.VMEM((ROWS, COLS), jnp.int32),
            pltpu.VMEM((2, ROWS, COLS), F32),
            pltpu.VMEM((2, ROWS, COLS), F32),
            pltpu.SemaphoreType.DMA((5,)),
            pltpu.SemaphoreType.DMA((16,)),
            pltpu.SemaphoreType.DMA((16,)),
        ],
        compiler_params=pltpu.CompilerParams(
            collective_id=0, has_side_effects=True, vmem_limit_bytes=24 * 1024 * 1024
        ),
        name="exchange",
    )(*(pltpu.with_memory_space_constraint(a, pltpu.HBM) for a in args))


def region(k):
    return (18 + 3 * k) // 8, (109 - 3 * k) // 8 + 1


def steps_kernel(coef, flow_in, pos_in, pair_in, sum_in, disp_out, vel_out, flow, pos, pair, near_sum):
    del flow_in, pos_in, pair_in, sum_in
    k = 0
    while k < STEPS:
        first, last = region(k)
        end = k + 1
        while end < STEPS and region(end) == (first, last):
            end += 1

        def advance(step, carry, starting=k == 0, first=first, last=last):
            scale = jnp.where(step == 0, 0.5 * TIME_STEP, TIME_STEP).astype(F32) if starting else TIME_STEP
            for index in range(first, last, 2):
                move(pos, pair, near_sum, flow, scale, 8 * index, 16)
            for index in range(first, last, 2):
                spread(pos, 8 * index, 16)
            for index in range(first, last, 2):
                forces(pos, coef, pair, near_sum, 8 * index, 16)
            return carry

        lax.fori_loop(k, end, advance, 0)
        k = end
    for component in range(2):
        disp_out[component] = pos[component, 0, 0, OWN]
    first, last = region(STEPS)
    for index in range(first, last, 2):
        move(pos, pair, near_sum, flow, 0.5 * TIME_STEP, 8 * index, 16, last=True)
    for component in range(2):
        vel_out[component] = flow[component, 0, OWN]


def run_steps(flow, pos, coef, pair, near_sum):
    vmem = pl.BlockSpec(memory_space=pltpu.VMEM)
    out = jax.ShapeDtypeStruct((2, ROWS, COLS), F32)
    arrays = (coef, flow, pos, pair, near_sum)
    return pl.pallas_call(
        steps_kernel,
        out_shape=(out, out, *(pltpu.VMEM(shape, F32) for shape in (FLOW, POS, PAIR, SUM))),
        in_specs=[vmem] * len(arrays),
        out_specs=(vmem,) * 6,
        input_output_aliases={1: 2, 2: 3, 3: 4, 4: 5},
        compiler_params=pltpu.CompilerParams(vmem_limit_bytes=24 * 1024 * 1024),
        name="steps",
    )(*(pltpu.with_memory_space_constraint(a, pltpu.VMEM) for a in arrays))[:2]


def solution(mesh):
    shape_x, shape_y = mesh.shape["gx"], mesh.shape["gy"]

    def on_device(disp, vel, stiffness, body_force, bond_bits):
        started = exchange(shape_x, shape_y, disp, vel, stiffness, body_force, bond_bits)
        return run_steps(*started)

    plane, word = P("gx", "gy"), P(None, "gx", "gy")
    return jax.shard_map(
        on_device, mesh=mesh, in_specs=(word, word, plane, word, word), out_specs=(word, word), check_vma=False
    )
```

```python
import functools
import math

import jax
import jax.numpy as jnp
from jax import lax
from jax.experimental import pallas as pl
from jax.experimental.pallas import tpu as pltpu
from jax.sharding import PartitionSpec as P

STEPS = 10
TIME_STEP = 0.04
ROWS = 32
COLS = 128
BASE = 48
TALL = 128
SIDE = 96
TINY = 1.2e-38
MESH = pl.DeviceIdType.MESH
OWN = pl.ds(BASE, ROWS)
WEST = [0, 32, 64, 96]
EAST = [96, 0, 32, 64]


def upper_shell():
    upper = []
    for row_step in range(0, 4):
        for col_step in range(-3, 4):
            if row_step * row_step + col_step * col_step <= 9 and (row_step > 0 or col_step > 0):
                upper.append((row_step, col_step))
    return upper


def half_shell():
    bonds = []
    for index, (row_step, col_step) in enumerate(upper_shell()):
        if col_step >= 0:
            bonds.append((row_step, col_step, index, False))
        else:
            bonds.append((-row_step, -col_step, index, True))
    return sorted(bonds, key=lambda bond: (bond[1], bond[0]))


BONDS = half_shell()


def lanes_of(shape):
    return lax.broadcasted_iota(jnp.int32, shape, len(shape) - 1)


def ahead(first, second, step):
    inside = lanes_of(first.shape) < COLS - step
    a, b = pltpu.roll(first, COLS - step, 1), pltpu.roll(second, COLS - step, 1)
    return jnp.where(inside, a, b), jnp.where(inside, b, a)


def behind(first, second, step):
    if step == 0:
        return first, second
    inside = lanes_of(first.shape) >= step
    a, b = pltpu.roll(first, step, 1), pltpu.roll(second, step, 1)
    return jnp.where(inside, a, b), jnp.where(inside, b, a)


def spread(pos, start, chunk):
    rows = pl.ds(start, chunk)
    for component in range(2):
        first, second = pos[component, 0, 0, rows], pos[component, 0, 1, rows]
        for step in range(1, 4):
            a, b = ahead(first, second, step)
            pos[component, step, 0, rows] = a + float(step) if component else a
            pos[component, step, 1, rows] = b + float(step) if component else b


def forces(pos, coef, pair, near_sum, start, chunk):
    rows = pl.ds(start, chunk)
    for tile in range(2):
        x, y = pos[0, 0, tile, rows], pos[1, 0, tile, rows]
        from_row = {row_step: x - float(row_step) if row_step else x for row_step in range(-2, 4)}
        sum_x = sum_y = None
        for j, (row_step, col_step, _, _) in enumerate(BONDS):
            there = pl.ds(start + row_step, chunk)
            dx = pos[0, col_step, tile, there] - from_row[row_step]
            dy = pos[1, col_step, tile, there] - y
            square = jnp.maximum(dx * dx + dy * dy, TINY)
            inverse_length = 1.0 / math.sqrt(row_step * row_step + col_step * col_step)
            weight = coef[j, tile, rows] * (inverse_length - lax.rsqrt(square))
            fx, fy = weight * dx, weight * dy
            pair[j, 0, tile, rows] = fx
            pair[j, 1, tile, rows] = fy
            sum_x = fx if sum_x is None else sum_x + fx
            sum_y = fy if sum_y is None else sum_y + fy
        near_sum[0, tile, rows] = sum_x
        near_sum[1, tile, rows] = sum_y


def force_loop(k, pos, coef, pair, near_sum):
    first, last = (15 + 3 * k) // 8, (111 - 3 * k) // 8 + 1

    def force_chunk(i, carry):
        forces(pos, coef, pair, near_sum, pl.multiple_of(8 * (first + 2 * i), 8), 16)
        return carry

    lax.fori_loop(0, (last - first + 1) // 2, force_chunk, 0)


def move(pos, pair, near_sum, flow, scale, start, chunk, last=False):
    rows = pl.ds(start, chunk)
    for component in range(2):
        total = [near_sum[component, 0, rows], near_sum[component, 1, rows]]
        for col_step in range(4):
            sums = []
            for tile in range(2):
                part = None
                for j, (row_step, step, _, _) in enumerate(BONDS):
                    if step == col_step:
                        value = pair[j, component, tile, pl.ds(start - row_step, chunk)]
                        part = value if part is None else part + value
                sums.append(part)
            back = behind(sums[0], sums[1], col_step)
            total = [total[0] - back[0], total[1] - back[1]]
        for tile in range(1 if last else 2):
            speed = flow[component, tile, rows] + scale * (total[tile] + flow[2 + component, tile, rows])
            flow[component, tile, rows] = speed
            if not last:
                pos[component, 0, tile, rows] = pos[component, 0, tile, rows] + TIME_STEP * speed


def packed(fields, start, groups):
    lanes = lanes_of((ROWS, COLS))
    total = None
    for field, group in zip(fields, groups, strict=True):
        moved = pltpu.roll(field, (group - start) % COLS, 1) if group != start else field
        total = moved if total is None else jnp.where((lanes >= group) & (lanes < group + 32), moved, total)
    return total


def beside(right, left, word, field, rows):
    lanes = lanes_of((8, COLS))
    at_right, at_left = WEST[field], EAST[field]
    value = jnp.where((lanes >= at_left) & (lanes < at_left + 32), left[word, rows], 0.0)
    value = jnp.where((lanes >= at_right) & (lanes < at_right + 32), right[word, rows], value)
    return pltpu.roll(value, -at_right % COLS, 1) if at_right else value


def begin(near, pos, stiff, flags, tiles):
    for index in tiles:
        rows = pl.ds(8 * index, 8)
        x, y, k = (near[field, rows] for field in range(3))
        bits = near[3, rows].astype(jnp.int32)
        pos[0, 0, 0, rows] = x
        pos[1, 0, 0, rows] = y
        stiff[0, 0, rows] = k
        flags[0, 0, rows] = bits
        for step in range(1, 4):
            pos[0, step, 0, rows] = pltpu.roll(x, COLS - step, 1)
            pos[1, step, 0, rows] = pltpu.roll(y, COLS - step, 1)
            stiff[step, 0, rows] = pltpu.roll(k, COLS - step, 1)
        for step in range(1, 3):
            flags[step, 0, rows] = pltpu.roll(bits, COLS - step, 1)


def finish(left, right, pos, coef, stiff, flags):
    lanes8 = lanes_of((8, COLS))
    zeros = jnp.zeros((8, COLS), jnp.float32)
    for index in range(1, 15):
        rows = pl.ds(8 * index, 8)
        others = [zeros] * 4
        if 2 <= index < 14:
            side = pl.ds(8 * index - 16, 8)
            for field in range(4):
                value = beside(right, left, 0, field, side)
                if 6 <= index < 10:
                    far_right = pltpu.roll(right[1, side], (32 - (WEST[field] + 30)) % COLS, 1)
                    far_left = pltpu.roll(left[1, side], (95 - (EAST[field] + 1)) % COLS, 1)
                    value = jnp.where(lanes8 == 32, far_right, jnp.where(lanes8 == 95, far_left, value))
                others[field] = value
        pos[0, 0, 1, rows] = others[0]
        pos[1, 0, 1, rows] = others[1]
        stiff[0, 1, rows] = others[2]
        flags[0, 1, rows] = others[3].astype(jnp.int32)

    def complete(ref, where, step, rows, bias):
        inside = lanes8 < COLS - step
        own, other = ref[(*where, step, 0, rows)], pltpu.roll(ref[(*where, 0, 1, rows)], COLS - step, 1)
        first, second = jnp.where(inside, own, other), jnp.where(inside, other, own)
        ref[(*where, step, 0, rows)] = first + bias if bias else first
        ref[(*where, step, 1, rows)] = second + bias if bias else second

    for index in range(1, 15):
        rows = pl.ds(8 * index, 8)
        for step in range(1, 4):
            complete(pos, (0,), step, rows, 0.0)
            complete(pos, (1,), step, rows, float(step))
            complete(stiff, (), step, rows, 0.0)
        for step in range(1, 3):
            complete(flags, (), step, rows, 0)

    def set_coefs(index, carry):
        start = pl.multiple_of(8 * index, 8)
        rows = pl.ds(start, 8)
        for tile in range(2):
            itself = stiff[0, tile, rows]
            bits = flags[0, tile, rows]
            for j, (row_step, col_step, bit, far) in enumerate(BONDS):
                there = pl.ds(start + row_step, 8)
                word = flags[col_step, tile, there] if far else bits
                value = 0.5 * (itself + stiff[col_step, tile, there])
                coef[j, tile, rows] = jnp.where((word & (1 << bit)) != 0, value, 0.0)
        return carry

    lax.fori_loop(1, 15, set_coefs, 0)


def exchange_kernel(shape_x, shape_y, disp, vel, stiff_own, body, bits, flow, pos, coef, pair, near_sum,
                    near, left, right, stiff, flags, bits_own, to_west, to_east, local_sem, send_sem, recv_sem):
    gx, gy = lax.axis_index("gx"), lax.axis_index("gy")

    def neighbour(row_step, col_step):
        return (
            lax.rem(gx + row_step + shape_x, shape_x),
            lax.rem(gy + col_step + shape_y, shape_y),
        )

    around = [(-1, -1), (-1, 1), (1, -1), (1, 1), (-1, 0), (1, 0), (0, -1), (0, 1), (-2, 0), (2, 0)]
    barrier = pltpu.get_barrier_semaphore()
    for step in around:
        pl.semaphore_signal(barrier, inc=1, device_id=neighbour(*step), device_id_type=MESH)

    local = [
        pltpu.make_async_copy(bits.at[0], bits_own, local_sem.at[0]),
        pltpu.make_async_copy(disp, near.at[pl.ds(0, 2), OWN], local_sem.at[1]),
        pltpu.make_async_copy(stiff_own, near.at[2, OWN], local_sem.at[2]),
        pltpu.make_async_copy(vel, flow.at[pl.ds(0, 2), 0, OWN], local_sem.at[3]),
        pltpu.make_async_copy(body, flow.at[pl.ds(2, 2), 0, OWN], local_sem.at[4]),
    ]
    for copy in local:
        copy.start()
    zeros = jnp.zeros((8, COLS), jnp.float32)
    for index in (0, 15):
        rows = pl.ds(8 * index, 8)
        for step in range(4):
            for tile in range(2):
                pos[0, step, tile, rows] = zeros
                pos[1, step, tile, rows] = zeros
                stiff[step, tile, rows] = zeros
        for step in range(3):
            for tile in range(2):
                flags[step, tile, rows] = jnp.zeros((8, COLS), jnp.int32)
    for copy in local:
        copy.wait()
    near[3, OWN] = bits_own[...].astype(jnp.float32)

    first_four = [near[field, OWN] for field in range(4)]
    last_four = [flow[field, 0, OWN] for field in range(4)]
    lanes = lanes_of((ROWS, COLS))
    to_west[0] = packed(first_four, 0, WEST)
    to_east[0] = packed(first_four, 96, EAST)
    west, east = packed(last_four, 0, WEST), packed(last_four, 96, EAST)
    for field in range(4):
        at_west, at_east = WEST[field] + 30, EAST[field] + 1
        west = jnp.where(lanes == at_west, pltpu.roll(first_four[field], (at_west - 32) % COLS, 1), west)
        east = jnp.where(lanes == at_east, pltpu.roll(first_four[field], (at_east - 95) % COLS, 1), east)
    to_west[1] = west
    to_east[1] = east
    begin(near, pos, stiff, flags, range(6, 10))

    pl.semaphore_wait(barrier, len(around))

    four = pl.ds(0, 4)
    plan = [
        (near.at[four, OWN], near.at[four, pl.ds(BASE + ROWS, ROWS)], (-1, 0)),
        (near.at[four, OWN], near.at[four, pl.ds(BASE - ROWS, ROWS)], (1, 0)),
        (to_west.at[0], right.at[0, pl.ds(64, 32)], (-1, -1)),
        (to_east.at[0], left.at[0, pl.ds(64, 32)], (-1, 1)),
        (to_west.at[0], right.at[0, pl.ds(0, 32)], (1, -1)),
        (to_east.at[0], left.at[0, pl.ds(0, 32)], (1, 1)),
        (to_west, right.at[:, pl.ds(32, 32)], (0, -1)),
        (to_east, left.at[:, pl.ds(32, 32)], (0, 1)),
        (near.at[four, pl.ds(BASE, 8)], near.at[four, pl.ds(BASE + 64, 8)], (-2, 0)),
        (near.at[four, pl.ds(BASE + 24, 8)], near.at[four, pl.ds(BASE - 40, 8)], (2, 0)),
        (to_west.at[1], right.at[1, pl.ds(64, 32)], (-1, -1)),
        (to_east.at[1], left.at[1, pl.ds(64, 32)], (-1, 1)),
        (to_west.at[1], right.at[1, pl.ds(0, 32)], (1, -1)),
        (to_east.at[1], left.at[1, pl.ds(0, 32)], (1, 1)),
        (flow.at[:, 0, OWN], flow.at[:, 0, pl.ds(BASE + ROWS, ROWS)], (-1, 0)),
        (flow.at[:, 0, OWN], flow.at[:, 0, pl.ds(BASE - ROWS, ROWS)], (1, 0)),
    ]
    copies = [
        pltpu.make_async_remote_copy(
            src_ref=source,
            dst_ref=target,
            send_sem=send_sem.at[index],
            recv_sem=recv_sem.at[index],
            device_id=neighbour(*step),
            device_id_type=MESH,
        )
        for index, (source, target, step) in enumerate(plan)
    ]
    order = [2, 3, 4, 5, 0, 1, 6, 7, 8, 9, 10, 11, 12, 13]
    for index in order:
        copies[index].start()
    for index in (0, 1):
        copies[index].wait_send()
    for copy in copies[14:]:
        copy.start()
    for index in (0, 1, 8, 9):
        copies[index].wait_recv()
    begin(near, pos, stiff, flags, [*range(1, 6), *range(10, 15)])
    for copy in copies[2:8]:
        copy.wait_recv()
    finish(left, right, pos, coef, stiff, flags)
    force_loop(0, pos, coef, pair, near_sum)
    for copy in copies[10:14]:
        copy.wait_recv()
    lanes8 = lanes_of((8, COLS))
    for index in range(2, 14):
        rows = pl.ds(8 * index, 8)
        side = pl.ds(8 * index - 16, 8)
        for field in range(4):
            value = beside(right, left, 1, field, side)
            flow[field, 1, rows] = jnp.where((lanes8 < 30) | (lanes8 >= 98), value, 0.0)
    for copy in copies[14:]:
        copy.wait_recv()
    for copy in copies[2:]:
        copy.wait_send()


F32 = jnp.float32
POS = (2, 4, 2, TALL, COLS)
PAIR = (14, 2, 2, TALL, COLS)
SUM = (2, 2, TALL, COLS)
FLOW = (4, 2, TALL, COLS)


def exchange(shape_x, shape_y, *args):
    hbm = pl.BlockSpec(memory_space=pltpu.HBM)
    vmem = pl.BlockSpec(memory_space=pltpu.VMEM)
    shapes = (FLOW, POS, (14, 2, TALL, COLS), PAIR, SUM)
    return pl.pallas_call(
        functools.partial(exchange_kernel, shape_x, shape_y),
        out_shape=tuple(pltpu.VMEM(shape, F32) for shape in shapes),
        in_specs=[hbm] * 5,
        out_specs=(vmem,) * len(shapes),
        scratch_shapes=[
            pltpu.VMEM((4, TALL, COLS), F32),
            pltpu.VMEM((2, SIDE, COLS), F32),
            pltpu.VMEM((2, SIDE, COLS), F32),
            pltpu.VMEM((4, 2, TALL, COLS), F32),
            pltpu.VMEM((3, 2, TALL, COLS), jnp.int32),
            pltpu.VMEM((ROWS, COLS), jnp.int32),
            pltpu.VMEM((2, ROWS, COLS), F32),
            pltpu.VMEM((2, ROWS, COLS), F32),
            pltpu.SemaphoreType.DMA((5,)),
            pltpu.SemaphoreType.DMA((16,)),
            pltpu.SemaphoreType.DMA((16,)),
        ],
        compiler_params=pltpu.CompilerParams(
            collective_id=0, has_side_effects=True, vmem_limit_bytes=24 * 1024 * 1024
        ),
        name="exchange",
    )(*(pltpu.with_memory_space_constraint(a, pltpu.HBM) for a in args))


def region(k):
    return (18 + 3 * k) // 8, (109 - 3 * k) // 8 + 1


def steps_kernel(coef, flow_in, pos_in, pair_in, sum_in, disp_out, vel_out, flow, pos, pair, near_sum, sent):
    del flow_in, pos_in, pair_in, sum_in
    leave = pltpu.make_async_copy(pos.at[:, 0, 0, OWN], disp_out, sent)
    k = 0
    while k < STEPS:
        first, last = region(k)
        end = k + 1
        while end < STEPS - 1 and region(end) == (first, last):
            end += 1

        def advance(step, carry, starting=k == 0, ending=end == STEPS, first=first, last=last):
            scale = jnp.where(step == 0, 0.5 * TIME_STEP, TIME_STEP).astype(F32) if starting else TIME_STEP
            for index in range(first, last, 2):
                move(pos, pair, near_sum, flow, scale, 8 * index, 16)
            if ending:
                leave.start()
            for index in range(first, last, 2):
                spread(pos, 8 * index, 16)
            for index in range(first, last, 2):
                forces(pos, coef, pair, near_sum, 8 * index, 16)
            return carry

        if end == STEPS:
            advance(k, 0)
        else:
            lax.fori_loop(k, end, advance, 0)
        k = end
    first, last = region(STEPS)
    for index in range(first, last, 2):
        move(pos, pair, near_sum, flow, 0.5 * TIME_STEP, 8 * index, 16, last=True)
    for component in range(2):
        vel_out[component] = flow[component, 0, OWN]
    leave.wait()


def run_steps(flow, pos, coef, pair, near_sum):
    vmem = pl.BlockSpec(memory_space=pltpu.VMEM)
    out = jax.ShapeDtypeStruct((2, ROWS, COLS), F32)
    arrays = (coef, flow, pos, pair, near_sum)
    return pl.pallas_call(
        steps_kernel,
        out_shape=(out, out, *(pltpu.VMEM(shape, F32) for shape in (FLOW, POS, PAIR, SUM))),
        in_specs=[vmem] * len(arrays),
        out_specs=(pl.BlockSpec(memory_space=pltpu.HBM), *(vmem,) * 5),
        scratch_shapes=[pltpu.SemaphoreType.DMA],
        input_output_aliases={1: 2, 2: 3, 3: 4, 4: 5},
        compiler_params=pltpu.CompilerParams(vmem_limit_bytes=24 * 1024 * 1024),
        name="steps",
    )(*(pltpu.with_memory_space_constraint(a, pltpu.VMEM) for a in arrays))[:2]


def solution(mesh):
    shape_x, shape_y = mesh.shape["gx"], mesh.shape["gy"]

    def on_device(disp, vel, stiffness, body_force, bond_bits):
        started = exchange(shape_x, shape_y, disp, vel, stiffness, body_force, bond_bits)
        return run_steps(*started)

    plane, word = P("gx", "gy"), P(None, "gx", "gy")
    return jax.shard_map(
        on_device, mesh=mesh, in_specs=(word, word, plane, word, word), out_specs=(word, word), check_vma=False
    )
```
